32 devices in a mesh: groups: 2 (over x), expert: 4 (over y, core), dp: 4 (over z).
Axes of the slice: x: 2, y: 2, z: 4, core: 2. Of those that a mesh axis runs over, the one named last changes fastest.
Arguments:
- tokens: bfloat16 [4096, 2048], P(('groups', 'expert', 'dp')), parts along dimension 0, may hold values from -6 to 6
- out_grad: bfloat16 [4096, 2048], P(('groups', 'expert', 'dp')), parts along dimension 0, may hold values from -6 to 6
- routes: int32 [4096, 2], P(('groups', 'expert', 'dp')), parts along dimension 0, may hold values from 0 to 3, all different within a row; in each aligned block of 128 rows (0 to 127, 128 to 255, ...) at most 128 rows name the same one
- route_gates: bfloat16 [4096, 2], P(('groups', 'expert', 'dp')), parts along dimension 0, may hold values from 0.049804688 to 1
- w_gate: bfloat16 [4, 2048, 768], P('expert'), may hold values from -0.125 to 0.125
- w_up: bfloat16 [4, 2048, 768], P('expert'), may hold values from -0.125 to 0.125
- w_down: bfloat16 [4, 768, 2048], P('expert'), may hold values from -0.21875 to 0.21875
Outputs:
- grad_tokens: bfloat16 [4096, 2048], P(('groups', 'expert', 'dp')), parts along dimension 0
- grad_gates: bfloat16 [4096, 2], P(('groups', 'expert', 'dp')), parts along dimension 0
- grad_gate: bfloat16 [8, 2048, 768], P(('groups', 'expert'), 'dp'), parts along dimension 0
- grad_up: bfloat16 [8, 2048, 768], P(('groups', 'expert'), 'dp'), parts along dimension 0
- grad_down: bfloat16 [8, 768, 2048], P(('groups', 'expert'), None, 'dp'), parts along dimension 0
The draws below stay inside these ranges and needn't reach their ends.
There are 2 independent parts, one for each index of `groups`. The reference program is written for one: setup_inputs(seed, part) draws one part's arguments, and reference() takes and returns one part's arrays. A program takes and returns all parts, laid end to end along the dimension named above; an argument that names none is the same for every part. Nothing has to cross between parts.
Inputs may be any that keep to these rules, and one draw needn't show every extreme that they name: `routes`: each token names 2 different experts. Within the 128 rows of one device no expert is named more than 128 times, and in every draw some expert is named exactly 128 times by the rows of some device.
All inputs are finite; a program needn't handle non-finite values.
Results may differ from the reference program's by a relative error of at most 0.0059.
Values may be sent and summed in bfloat16 or wider, within the bound.
A program may use at most 128 MiB of HBM per device.

```python
import math
import jax
import jax.numpy as jnp
import numpy as np
from jax import lax

D = 2048
H = 768
TOK_DEV = 128
TOP = 2
EXPERTS = 4
CAP = 128
TOKENS = 2048
N_EXPERT = 4
N_DP = 4


def block_levels(key, dims, pieces, least, top_value):
    loudness = 1.0
    for dim, blocks in pieces:
        heights = jax.random.uniform(jax.random.fold_in(jax.random.fold_in(key, 6), dim), (blocks,), jnp.float32, least / len(pieces), top_value / len(pieces))
        loudness = loudness * jnp.repeat(jnp.exp(heights), dims[dim] // blocks).reshape((-1,) + (1,) * (len(dims) - 1 - dim))
    return loudness


def routed_block(own_key, own, number, rows, number_of, top, most, lean):
    ranking = jax.random.permutation(own_key, number_of)
    heavy_load, usual = load_shares(number_of, rows * top, most, lean, True), load_shares(number_of, rows * top, most, lean, False)
    places = jnp.arange(number_of)

    def named(sizes, turn):
        used = int((sizes > 0).sum())
        fixed = max(1, used // 4)
        shifted = fixed + (places - fixed + turn * (used - fixed)) % max(1, number_of - fixed)
        return jnp.zeros((number_of,), jnp.int32).at[ranking[jnp.where(places < fixed, places, shifted)]].set(jnp.asarray(sizes, jnp.int32))

    sizes = jnp.where(number % 4 == 0, named(heavy_load, number // 4), named(usual, number - number // 4 - 1))
    mixed = jax.random.permutation(jax.random.fold_in(own, 3), number_of)
    source_of, receiver = mixed[0:number_of // 2 * 2:2], mixed[1:number_of // 2 * 2:2]
    margin = jnp.minimum(sizes[source_of] - 1, most - sizes[receiver]) // 2
    margin = jnp.where((source_of == ranking[0]) | (receiver == ranking[0]) | (sizes[receiver] == 0), 0, jnp.maximum(margin, 0))
    shifted = jax.random.randint(jax.random.fold_in(own, 4), (number_of // 2,), 0, 1 << 20) % (margin + 1)
    sizes = sizes.at[source_of].add(-shifted).at[receiver].add(shifted)
    members = jnp.searchsorted(jnp.cumsum(sizes), jnp.arange(rows * top), side="right").astype(jnp.int32)
    grid = members.reshape(top, rows).T
    grid = grid[jax.random.permutation(jax.random.fold_in(own, 1), rows)]
    turn = jax.random.randint(jax.random.fold_in(own, 2), (rows, 1), 0, top)
    return jnp.take_along_axis(grid, (jnp.arange(top)[None, :] + turn) % top, axis=1)


def load_shares(number_of, total, limit, lean, full):
    weights = [(1 << 20) // math.isqrt(standing ** lean) + 1 for standing in range(1, number_of + 1)]
    largest = limit if full else min(limit, max(-(-total // number_of), total * weights[0] // sum(weights)))
    least = 1 if total - largest >= number_of - 1 else 0
    counts, surplus = [largest] + [least] * (number_of - 1), total - largest - least * (number_of - 1)
    while surplus > 0:
        movable = [i for i in range(1, number_of) if counts[i] < largest] or [i for i in range(1, number_of) if counts[i] < limit]
        pool, left = sum([weights[i] for i in movable]), surplus
        for i in movable:
            extra = min(limit - counts[i], max(1, left * weights[i] // pool), surplus)
            counts[i] = counts[i] + extra
            surplus = surplus - extra
    return np.array(counts)


def gaussian(key, extent, spread, reach, shards=(), held_as=jnp.bfloat16):
    loudness = block_levels(key, extent, shards, -0.22, 0.18) if shards else 1.0
    entries = jax.random.normal(key, extent, jnp.float32) * spread * loudness
    return jnp.minimum(jnp.maximum(entries, -reach), reach).astype(held_as)


def setup_inputs(seed: int = 0, part: int = 0) -> dict:
    key_list = jax.random.split(jax.random.key(seed), 8)
    part_keys = jax.random.split(jax.random.fold_in(key_list[7], part), 8)
    tokens = gaussian(part_keys[0], (TOKENS, D), 1.0, 6.0, ((0, 16),))
    out_grad = gaussian(part_keys[1], (TOKENS, D), 1.0, 6.0, ((0, 16),))
    routes_keys = jax.random.split(jax.random.fold_in(part_keys[2], 1), TOKENS // TOK_DEV)
    routes_turns = jax.random.permutation(jax.random.fold_in(part_keys[2], 3), TOKENS // TOK_DEV)
    routes = jax.vmap(lambda own, number: routed_block(jax.random.fold_in(part_keys[2], 2), own, number, TOK_DEV, EXPERTS, TOP, CAP, 2))(routes_keys, routes_turns).reshape((TOKENS, TOP))
    route_gates = jnp.clip(jnp.exp(math.log(1.0) - 2.9996462 * jax.random.uniform(part_keys[3], (TOKENS, TOP), jnp.float32) ** block_levels(part_keys[3], (TOKENS, TOP), ((0, 16),), -0.2, 0.2)), 0.049804688, 1.0).astype(jnp.bfloat16)
    w_gate = gaussian(key_list[4], (EXPERTS, D, H), D ** -0.5, 0.125, ((0, 4),))
    w_up = gaussian(key_list[5], (EXPERTS, D, H), D ** -0.5, 0.125, ((0, 4),))
    w_down = gaussian(key_list[6], (EXPERTS, H, D), H ** -0.5, 0.21875, ((0, 4),))
    return {"tokens": tokens, "out_grad": out_grad, "routes": routes, "route_gates": route_gates, "w_gate": w_gate, "w_up": w_up, "w_down": w_down}


def reference(tokens, out_grad, routes, route_gates, w_gate, w_up, w_down):
    route_total = TOKENS * TOP
    most_rows = N_EXPERT * N_DP * CAP
    flat_ids = routes.reshape(-1)
    flat_gates = route_gates.reshape(-1)

    def per_expert(carried, expert):
        route_dx, route_dg = carried
        chosen = flat_ids == expert
        picked = jnp.nonzero(chosen, size=most_rows, fill_value=route_total)[0].astype(jnp.int32)
        valid_row = picked < route_total
        safe_route = jnp.minimum(picked, route_total - 1)
        token_index = safe_route // TOP
        token_rows = jnp.where(valid_row[:, None], tokens[token_index], jnp.zeros((), tokens.dtype))
        grad_rows = out_grad[token_index]
        gate_rows = jnp.where(valid_row, flat_gates[safe_route], jnp.zeros((), route_gates.dtype))
        gate_mat = lax.dynamic_index_in_dim(w_gate, expert, 0, keepdims=False)
        up_mat = lax.dynamic_index_in_dim(w_up, expert, 0, keepdims=False)
        down_mat = lax.dynamic_index_in_dim(w_down, expert, 0, keepdims=False)
        pre_gate = jnp.dot(token_rows, gate_mat, preferred_element_type=jnp.float32)
        pre_up = jnp.dot(token_rows, up_mat, preferred_element_type=jnp.float32)
        sigmoid_gate = jax.nn.sigmoid(pre_gate)
        activated = pre_gate * sigmoid_gate
        hidden = (activated * pre_up).astype(jnp.bfloat16)
        back_proj = jnp.dot(grad_rows, down_mat.T, preferred_element_type=jnp.float32)
        expert_output = jnp.dot(hidden, down_mat, preferred_element_type=jnp.float32)
        gate_grad = jnp.sum(expert_output * grad_rows.astype(jnp.float32), axis=1).astype(jnp.bfloat16)
        gate_scale = gate_rows.astype(jnp.float32)[:, None]
        scaled_back = gate_scale * back_proj
        grad_pre_gate = (scaled_back * pre_up * sigmoid_gate * (1.0 + pre_gate * (1.0 - sigmoid_gate))).astype(jnp.bfloat16)
        grad_pre_up = (scaled_back * activated).astype(jnp.bfloat16)
        route_grad = (jnp.dot(grad_pre_gate, gate_mat.T, preferred_element_type=jnp.float32)
                      + jnp.dot(grad_pre_up, up_mat.T, preferred_element_type=jnp.float32)).astype(jnp.bfloat16)
        scaled_grad = (gate_scale * grad_rows.astype(jnp.float32)).astype(jnp.bfloat16)
        grad_g = jnp.dot(token_rows.T, grad_pre_gate, preferred_element_type=jnp.float32).astype(jnp.bfloat16)
        grad_u = jnp.dot(token_rows.T, grad_pre_up, preferred_element_type=jnp.float32).astype(jnp.bfloat16)
        grad_d = jnp.dot(hidden.T, scaled_grad, preferred_element_type=jnp.float32).astype(jnp.bfloat16)
        route_dx = route_dx.at[picked].set(route_grad, mode="drop")
        route_dg = route_dg.at[picked].set(gate_grad, mode="drop")
        return (route_dx, route_dg), (grad_g, grad_u, grad_d)

    start_state = (jnp.zeros((route_total, D), jnp.bfloat16), jnp.zeros((route_total,), jnp.bfloat16))
    (route_dx, route_dg), grads = lax.scan(per_expert, start_state, jnp.arange(EXPERTS, dtype=jnp.int32))
    grad_tokens = jnp.sum(route_dx.reshape(TOKENS, TOP, D).astype(jnp.float32), axis=1).astype(jnp.bfloat16)
    grad_gates = route_dg.reshape(TOKENS, TOP)
    return grad_tokens, grad_gates, grads[0], grads[1], grads[2]
```

```python
import functools
import jax
import jax.numpy as jnp
from jax import lax
from jax.experimental import pallas as pl
from jax.experimental.pallas import tpu as pltpu
from jax.sharding import PartitionSpec as P

MESH = pl.DeviceIdType.MESH
F32 = jnp.float32
BF16 = jnp.bfloat16
LANES = 128
PIECES = ((0, 32, "both"), (32, 48, "own"), (80, 48, "own"))
H_TILE = 256
D_TILE = 256


def dot_nt(a, b):
    return lax.dot_general(a, b, (((1,), (1,)), ((), ())), preferred_element_type=F32)


def dot_tn(a, b):
    return lax.dot_general(a, b, (((0,), (0,)), ((), ())), preferred_element_type=F32)


def layer_kernel(
    n_expert, n_dp,
    tok_ref, og_ref, routes_ref, gates_ref, wg_hbm, wu_hbm, wd_hbm,
    gtok_out, ggate_out, dg_out, du_out, dd_out,
    blocks, wg, wu, wd, acc_g, acc_u, acc_d, keep_g, keep_u, gate_sum, give, got,
    load_sem, send_sem, recv_sem, give_sem, got_sem,
):
    rows = tok_ref.shape[0]
    width = tok_ref.shape[1]
    hidden_width = wg.shape[1]
    group_rows = n_expert * rows
    shard = width // n_dp
    e = lax.axis_index("expert")
    z = lax.axis_index("dp")
    core = e % 2
    sibling = e + 1 - 2 * core
    across = (e + 2) % 4

    def own_rows(expert, start, count):
        return pl.ds(pl.multiple_of(expert * rows + start, 16), count)

    loads = [
        pltpu.make_async_copy(tok_ref, blocks.at[z, own_rows(e, 0, rows), 0:width], load_sem.at[0]),
        pltpu.make_async_copy(og_ref, blocks.at[z, own_rows(e, 0, rows), width:2 * width], load_sem.at[1]),
        pltpu.make_async_copy(wg_hbm.at[0], wg, load_sem.at[2]),
        pltpu.make_async_copy(wu_hbm.at[0], wu, load_sem.at[3]),
        pltpu.make_async_copy(wd_hbm.at[0], wd, load_sem.at[4]),
    ]
    for load in loads:
        load.start()

    barrier = pltpu.get_barrier_semaphore()
    for j in (1, 2, 3):
        pl.semaphore_signal(barrier, inc=1, device_id={"expert": (e + j) % 4}, device_id_type=MESH)

    @pl.when(z > 0)
    def _():
        pl.semaphore_signal(barrier, inc=1, device_id={"dp": z - 1}, device_id_type=MESH)

    @pl.when(z < n_dp - 1)
    def _():
        pl.semaphore_signal(barrier, inc=1, device_id={"dp": z + 1}, device_id_type=MESH)

    lane = lax.broadcasted_iota(jnp.int32, (rows, LANES), 1)
    spread = jnp.zeros((rows, LANES), F32)
    for k in range(2):
        spread += jnp.where(
            lane == routes_ref[:, k:k + 1], gates_ref[:, k:k + 1].astype(F32), 0.0
        )
    blocks[z, own_rows(e, 0, rows), 2 * width:2 * width + LANES] = spread.astype(BF16)

    pl.semaphore_wait(barrier, 3 + jnp.minimum(z, 1) + jnp.minimum(n_dp - 1 - z, 1))

    loads[0].wait()
    loads[1].wait()

    def source_of(step):
        half = z // 2
        near = z + half * (3 - 2 * z)
        last = step // 3
        inner = last * 3 + (1 - last) * ((step + 1) % 3)
        place = (1 - near) * step + near * inner
        return place + half * (3 - 2 * place)

    def piece_copy(kind, src, expert, other, p, target):
        start, count, _ = PIECES[p]
        ref = blocks.at[src, own_rows(expert, start, count), :]
        return pltpu.make_async_remote_copy(
            src_ref=ref, dst_ref=ref,
            send_sem=send_sem.at[kind, src, other, p],
            recv_sem=recv_sem.at[src, expert, p],
            device_id=target, device_id_type=MESH,
        )

    def each_send(step, src, other, p, act):
        expert = across if other else e
        both = PIECES[p][2] == "both"
        if both or not other:
            @pl.when(jnp.logical_and(src <= z, z < n_dp - 1))
            def _():
                act(piece_copy(0, src, expert, other, p, {"dp": z + 1}))

            @pl.when(jnp.logical_and(src >= z, z > 0))
            def _():
                act(piece_copy(1, src, expert, other, p, {"dp": z - 1}))
        if not other:
            if both:
                @pl.when(step == 0)
                def _():
                    act(piece_copy(2, src, expert, other, p, {"expert": across}))
            else:
                act(piece_copy(2, src, expert, other, p, {"expert": across}))
        act(piece_copy(3, src, expert, other, p, {"expert": sibling}))

    def move(step):
        src = source_of(step)
        for other in (0, 1):
            expert = across if other else e
            for p in range(len(PIECES)):
                arrival = piece_copy(3, src, expert, other, p, {"expert": sibling})
                if other:
                    arrival.wait_recv()
                else:
                    @pl.when(step > 0)
                    def _():
                        arrival.wait_recv()
                each_send(step, src, other, p, lambda c: c.start())

    def await_sibling(step):
        src = source_of(step)
        for other in (0, 1):
            expert = (sibling + 2) % 4 if other else sibling
            for p in range(len(PIECES)):
                piece_copy(3, src, expert, other, p, {"expert": sibling}).wait_recv()

    def compute(step):
        src = source_of(step)
        wide = lax.broadcasted_iota(jnp.int32, (group_rows, LANES), 1)
        gate = jnp.sum(
            jnp.where(wide == e, blocks[src, :, 2 * width:2 * width + LANES].astype(F32), 0.0),
            axis=1, keepdims=True,
        )
        mine = pl.ds(pl.multiple_of(z * shard, LANES), shard)
        mine_og = pl.ds(pl.multiple_of(width + z * shard, LANES), shard)
        gate_sum[...] = jnp.zeros_like(gate_sum)

        def h_step(i, carry):
            hs = pl.ds(pl.multiple_of(i * H_TILE, H_TILE), H_TILE)
            x = blocks[src, :, 0:width]
            pre_gate = jnp.dot(x, wg[:, hs], preferred_element_type=F32)
            pre_up = jnp.dot(x, wu[:, hs], preferred_element_type=F32)
            back = dot_nt(blocks[src, :, width:2 * width], wd[hs, :])
            sig = jax.nn.sigmoid(pre_gate)
            act = pre_gate * sig
            hidden = (act * pre_up).astype(BF16)
            gate_sum[...] += jnp.sum(hidden.astype(F32) * back, axis=1, keepdims=True)
            scaled = gate * back
            grad_g = (scaled * pre_up * sig * (1.0 + pre_gate * (1.0 - sig))).astype(BF16)
            grad_u = (scaled * act).astype(BF16)
            keep_g[:, hs] = grad_g
            keep_u[:, hs] = grad_u
            xs = blocks[src, :, mine]
            acc_g[:, hs] += dot_tn(xs, grad_g)
            acc_u[:, hs] += dot_tn(xs, grad_u)
            scaled_grad = (gate * blocks[src, :, mine_og].astype(F32)).astype(BF16)
            acc_d[hs, :] += dot_tn(hidden, scaled_grad)
            return carry

        lax.fori_loop(0, hidden_width // H_TILE, h_step, 0)

    def give_copy(j):
        return pltpu.make_async_remote_copy(
            src_ref=give.at[(e + j) % 4], dst_ref=got.at[j - 1],
            send_sem=give_sem.at[j - 1], recv_sem=got_sem.at[j - 1],
            device_id={"expert": (e + j) % 4}, device_id_type=MESH,
        )

    def route_back():
        def d_step(i, carry):
            ds = pl.ds(pl.multiple_of(i * D_TILE, D_TILE), D_TILE)
            total = dot_nt(keep_g[...], wg[ds, :]) + dot_nt(keep_u[...], wu[ds, :])
            give[:, :, ds] = total.astype(BF16).reshape(n_expert, rows, D_TILE)
            return carry

        lax.fori_loop(0, width // D_TILE, d_step, 0)
        give[:, :, width:width + LANES] = (
            jnp.broadcast_to(gate_sum[...], (group_rows, LANES))
            .astype(BF16).reshape(n_expert, rows, LANES)
        )
        for j in (1, 2, 3):
            give_copy(j).start()

    def one_step(step, carry):
        move(step)

        @pl.when(step == 0)
        def _():
            acc_g[...] = jnp.zeros_like(acc_g)
            acc_u[...] = jnp.zeros_like(acc_u)
            acc_d[...] = jnp.zeros_like(acc_d)
            for load in loads[2:]:
                load.wait()

        await_sibling(step)
        compute(step)

        @pl.when(step == 0)
        def _():
            route_back()

        return carry

    lax.fori_loop(0, n_dp, one_step, 0)

    for j in (1, 2, 3):
        give_copy(j).wait_recv()
    total = give[e, :, 0:width].astype(F32)
    for j in (1, 2, 3):
        total += got[j - 1, :, 0:width].astype(F32)
    gtok_out[...] = total.astype(BF16)
    picked = []
    for k in range(2):
        route = routes_ref[:, k:k + 1]
        value = jnp.where(route == e, give[e, :, width:width + LANES].astype(F32), 0.0)
        for j in (1, 2, 3):
            value += jnp.where(
                route == (e + 4 - j) % 4, got[j - 1, :, width:width + LANES].astype(F32), 0.0
            )
        picked.append(value)
    ggate_out[...] = jnp.where(lane == 0, picked[0], picked[1])[:, 0:2].astype(BF16)
    dg_out[0] = acc_g[...].astype(BF16)
    du_out[0] = acc_u[...].astype(BF16)
    dd_out[0] = acc_d[...].astype(BF16)

    def drain(step, carry):
        src = source_of(step)
        for other in (0, 1):
            for p in range(len(PIECES)):
                each_send(step, src, other, p, lambda c: c.wait_send())
        return carry

    lax.fori_loop(0, n_dp, drain, 0)
    for j in (1, 2, 3):
        give_copy(j).wait_send()


def gathered_body(tokens, out_grad, routes, route_gates, w_gate, w_up, w_down):
    n_expert, n_dp = lax.axis_size("expert"), lax.axis_size("dp")
    rows, width = tokens.shape
    hid = w_gate.shape[2]
    shard = width // n_dp
    group_rows = n_expert * rows
    vmem = pl.BlockSpec(memory_space=pltpu.VMEM)
    hbm = pl.BlockSpec(memory_space=pl.ANY)
    pieces = len(PIECES)
    return pl.pallas_call(
        functools.partial(layer_kernel, n_expert, n_dp),
        out_shape=(
            jax.ShapeDtypeStruct((rows, width), BF16),
            jax.ShapeDtypeStruct((rows, 2), BF16),
            jax.ShapeDtypeStruct((1, shard, hid), BF16),
            jax.ShapeDtypeStruct((1, shard, hid), BF16),
            jax.ShapeDtypeStruct((1, hid, shard), BF16),
        ),
        in_specs=[hbm, hbm, vmem, vmem, hbm, hbm, hbm],
        out_specs=(vmem,) * 5,
        scratch_shapes=[
            pltpu.VMEM((n_dp, group_rows, 2 * width + LANES), BF16),
            pltpu.VMEM((width, hid), BF16),
            pltpu.VMEM((width, hid), BF16),
            pltpu.VMEM((hid, width), BF16),
            pltpu.VMEM((shard, hid), F32),
            pltpu.VMEM((shard, hid), F32),
            pltpu.VMEM((hid, shard), F32),
            pltpu.VMEM((group_rows, hid), BF16),
            pltpu.VMEM((group_rows, hid), BF16),
            pltpu.VMEM((group_rows, 1), F32),
            pltpu.VMEM((n_expert, rows, width + LANES), BF16),
            pltpu.VMEM((n_expert - 1, rows, width + LANES), BF16),
            pltpu.SemaphoreType.DMA((5,)),
            pltpu.SemaphoreType.DMA((4, n_dp, 2, pieces)),
            pltpu.SemaphoreType.DMA((n_dp, n_expert, pieces)),
            pltpu.SemaphoreType.DMA((3,)),
            pltpu.SemaphoreType.DMA((3,)),
        ],
        compiler_params=pltpu.CompilerParams(
            collective_id=0, has_side_effects=True, vmem_limit_bytes=60 * 2**20
        ),
    )(tokens, out_grad, routes, route_gates, w_gate, w_up, w_down)


def expert_rows(token_rows, grad_rows, gate_rows, gate_mat, up_mat, down_mat):
    pre_gate = jnp.dot(token_rows, gate_mat, preferred_element_type=jnp.float32)
    pre_up = jnp.dot(token_rows, up_mat, preferred_element_type=jnp.float32)
    sigmoid_gate = jax.nn.sigmoid(pre_gate)
    activated = pre_gate * sigmoid_gate
    hidden = (activated * pre_up).astype(jnp.bfloat16)
    back_proj = jnp.einsum("rd,hd->rh", grad_rows, down_mat, preferred_element_type=jnp.float32)
    expert_output = jnp.dot(hidden, down_mat, preferred_element_type=jnp.float32)
    gate_grad = jnp.sum(expert_output * grad_rows.astype(jnp.float32), axis=1)
    gate_scale = gate_rows.astype(jnp.float32)[:, None]
    scaled_back = gate_scale * back_proj
    grad_pre_gate = (
        scaled_back * pre_up * sigmoid_gate * (1.0 + pre_gate * (1.0 - sigmoid_gate))
    ).astype(jnp.bfloat16)
    grad_pre_up = (scaled_back * activated).astype(jnp.bfloat16)
    route_grad = (
        jnp.einsum("rh,dh->rd", grad_pre_gate, gate_mat, preferred_element_type=jnp.float32)
        + jnp.einsum("rh,dh->rd", grad_pre_up, up_mat, preferred_element_type=jnp.float32)
    ).astype(jnp.bfloat16)
    scaled_grad = (gate_scale * grad_rows.astype(jnp.float32)).astype(jnp.bfloat16)
    return (
        route_grad,
        gate_grad.astype(jnp.bfloat16),
        grad_pre_gate,
        grad_pre_up,
        hidden,
        scaled_grad,
    )


def body(tokens, out_grad, routes, route_gates, w_gate, w_up, w_down):
    tok_count, top_count = routes.shape
    model_width = tokens.shape[1]
    experts_total = lax.axis_size("expert")
    route_count = tok_count * top_count
    capacity = 2 * route_count // experts_total
    slot_total = experts_total * capacity
    flat_ids = routes.reshape(-1)
    one_hot = (flat_ids[:, None] == jnp.arange(experts_total, dtype=jnp.int32)[None, :]).astype(
        jnp.int32
    )
    route_rank = jnp.sum(jnp.cumsum(one_hot, axis=0) * one_hot, axis=1) - 1
    slot_index = flat_ids * capacity + route_rank
    slot_owner = (
        jnp.full((slot_total,), route_count, jnp.int32)
        .at[slot_index]
        .set(jnp.arange(route_count, dtype=jnp.int32))
    )
    filled = slot_owner < route_count
    safe_owner = jnp.minimum(slot_owner, route_count - 1)
    token_pick = safe_owner // top_count
    zero_bf = jnp.zeros((), jnp.bfloat16)
    send_tokens = jnp.where(filled[:, None], tokens[token_pick], zero_bf).reshape(
        experts_total, capacity, model_width
    )
    send_grads = jnp.where(filled[:, None], out_grad[token_pick], zero_bf).reshape(
        experts_total, capacity, model_width
    )
    send_gates = jnp.where(filled, route_gates.reshape(-1)[safe_owner], zero_bf).reshape(
        experts_total, capacity
    )
    recv_tokens, recv_grads, recv_gates = (
        lax.all_to_all(send_tokens, "expert", split_axis=0, concat_axis=0, tiled=True),
        lax.all_to_all(send_grads, "expert", split_axis=0, concat_axis=0, tiled=True),
        lax.all_to_all(send_gates, "expert", split_axis=0, concat_axis=0, tiled=True),
    )
    slot_rows = recv_tokens.shape[0] * recv_tokens.shape[1]
    token_rows = recv_tokens.reshape(slot_rows, model_width)
    grad_rows = recv_grads.reshape(slot_rows, model_width)
    gate_rows = recv_gates.reshape(slot_rows)
    gate_mat = w_gate[0]
    up_mat = w_up[0]
    down_mat = w_down[0]
    route_grad, gate_grad, grad_pre_gate, grad_pre_up, hidden, scaled_grad = expert_rows(
        token_rows, grad_rows, gate_rows, gate_mat, up_mat, down_mat
    )
    back_grad, back_gate = (
        lax.all_to_all(
            route_grad.reshape(experts_total, capacity, model_width),
            "expert",
            split_axis=0,
            concat_axis=0,
            tiled=True,
        ),
        lax.all_to_all(
            gate_grad.reshape(experts_total, capacity),
            "expert",
            split_axis=0,
            concat_axis=0,
            tiled=True,
        ),
    )
    home_grad = back_grad.reshape(slot_total, model_width)[slot_index]
    grad_tokens = jnp.sum(
        home_grad.reshape(tok_count, top_count, model_width).astype(jnp.float32), axis=1
    ).astype(jnp.bfloat16)
    grad_gates = back_gate.reshape(slot_total)[slot_index].reshape(tok_count, top_count)
    term_gate = jnp.einsum(
        "rd,rh->dh", token_rows, grad_pre_gate, preferred_element_type=jnp.float32
    )
    term_up = jnp.einsum("rd,rh->dh", token_rows, grad_pre_up, preferred_element_type=jnp.float32)
    term_down = jnp.einsum("rh,rd->hd", hidden, scaled_grad, preferred_element_type=jnp.float32)
    shares = (
        lax.psum_scatter(term_gate, "dp", scatter_dimension=0, tiled=True),
        lax.psum_scatter(term_up, "dp", scatter_dimension=0, tiled=True),
        lax.psum_scatter(term_down, "dp", scatter_dimension=1, tiled=True),
    )
    grad_gate = shares[0].astype(jnp.bfloat16)[None]
    grad_up = shares[1].astype(jnp.bfloat16)[None]
    grad_down = shares[2].astype(jnp.bfloat16)[None]
    return (grad_tokens, grad_gates, grad_gate, grad_up, grad_down)


def solution(mesh):
    placed = (
        P(("groups", "expert", "dp"), None),
        P(("groups", "expert", "dp"), None),
        P(("groups", "expert", "dp"), None),
        P(("groups", "expert", "dp"), None),
        P("expert", None, None),
        P("expert", None, None),
        P("expert", None, None),
    )
    small = mesh.shape["expert"] == 4 and mesh.shape["dp"] == 4
    return jax.shard_map(
        gathered_body if small else body,
        mesh=mesh,
        in_specs=placed,
        out_specs=(
            P(("groups", "expert", "dp"), None),
            P(("groups", "expert", "dp"), None),
            P(("groups", "expert"), "dp", None),
            P(("groups", "expert"), "dp", None),
            P(("groups", "expert"), None, "dp"),
        ),
        check_vma=False,
    )
```

```python
import functools
import jax
import jax.numpy as jnp
from jax import lax
from jax.experimental import pallas as pl
from jax.experimental.pallas import tpu as pltpu
from jax.sharding import PartitionSpec as P

MESH = pl.DeviceIdType.MESH
F32 = jnp.float32
BF16 = jnp.bfloat16
LANES = 128
PIECES = ((0, 32, "both"), (32, 48, "own"), (80, 48, "own"))
H_TILE = 256
D_TILE = 256


def dot_nt(a, b):
    return lax.dot_general(a, b, (((1,), (1,)), ((), ())), preferred_element_type=F32)


def dot_tn(a, b):
    return lax.dot_general(a, b, (((0,), (0,)), ((), ())), preferred_element_type=F32)


def layer_kernel(
    n_expert, n_dp,
    tok_ref, og_ref, routes_ref, gates_ref, wg_hbm, wu_hbm, wd_hbm,
    gtok_out, ggate_out, dg_out, du_out, dd_out,
    blocks, wg, wu, wd, acc_g, acc_u, acc_d, keep_g, keep_u, gate_sum, give, got,
    load_sem, send_sem, recv_sem, give_sem, got_sem,
):
    rows = tok_ref.shape[0]
    width = tok_ref.shape[1]
    hidden_width = wg.shape[1]
    group_rows = n_expert * rows
    shard = width // n_dp
    e = lax.axis_index("expert")
    z = lax.axis_index("dp")
    core = e % 2
    sibling = e + 1 - 2 * core
    across = (e + 2) % 4

    def own_rows(expert, start, count):
        return pl.ds(pl.multiple_of(expert * rows + start, 16), count)

    loads = [
        pltpu.make_async_copy(tok_ref, blocks.at[z, own_rows(e, 0, rows), 0:width], load_sem.at[0]),
        pltpu.make_async_copy(og_ref, blocks.at[z, own_rows(e, 0, rows), width:2 * width], load_sem.at[1]),
        pltpu.make_async_copy(wg_hbm.at[0], wg, load_sem.at[2]),
        pltpu.make_async_copy(wu_hbm.at[0], wu, load_sem.at[3]),
        pltpu.make_async_copy(wd_hbm.at[0], wd, load_sem.at[4]),
    ]
    for load in loads:
        load.start()

    barrier = pltpu.get_barrier_semaphore()
    for j in (1, 2, 3):
        pl.semaphore_signal(barrier, inc=1, device_id={"expert": (e + j) % 4}, device_id_type=MESH)

    @pl.when(z > 0)
    def _():
        pl.semaphore_signal(barrier, inc=1, device_id={"dp": z - 1}, device_id_type=MESH)

    @pl.when(z < n_dp - 1)
    def _():
        pl.semaphore_signal(barrier, inc=1, device_id={"dp": z + 1}, device_id_type=MESH)

    lane = lax.broadcasted_iota(jnp.int32, (rows, LANES), 1)
    spread = jnp.zeros((rows, LANES), F32)
    for k in range(2):
        spread += jnp.where(
            lane == routes_ref[:, k:k + 1], gates_ref[:, k:k + 1].astype(F32), 0.0
        )
    blocks[z, own_rows(e, 0, rows), 2 * width:2 * width + LANES] = spread.astype(BF16)

    pl.semaphore_wait(barrier, 3 + jnp.minimum(z, 1) + jnp.minimum(n_dp - 1 - z, 1))

    loads[0].wait()
    loads[1].wait()

    def source_of(step):
        half = z // 2
        near = z + half * (3 - 2 * z)
        last = step // 3
        inner = last * 3 + (1 - last) * ((step + 1) % 3)
        place = (1 - near) * step + near * inner
        return place + half * (3 - 2 * place)

    def piece_copy(kind, src, expert, other, p, target):
        start, count, _ = PIECES[p]
        ref = blocks.at[src, own_rows(expert, start, count), :]
        return pltpu.make_async_remote_copy(
            src_ref=ref, dst_ref=ref,
            send_sem=send_sem.at[kind, src, other, p],
            recv_sem=recv_sem.at[src, expert, p],
            device_id=target, device_id_type=MESH,
        )

    def each_send(step, src, other, p, act):
        expert = across if other else e
        both = PIECES[p][2] == "both"
        if both or not other:
            @pl.when(jnp.logical_and(src <= z, z < n_dp - 1))
            def _():
                act(piece_copy(0, src, expert, other, p, {"dp": z + 1}))

            @pl.when(jnp.logical_and(src >= z, z > 0))
            def _():
                act(piece_copy(1, src, expert, other, p, {"dp": z - 1}))
        if not other:
            if both:
                @pl.when(step == 0)
                def _():
                    act(piece_copy(2, src, expert, other, p, {"expert": across}))
            else:
                act(piece_copy(2, src, expert, other, p, {"expert": across}))
        act(piece_copy(3, src, expert, other, p, {"expert": sibling}))

    def late(other, p):
        return other == 1 and PIECES[p][2] == "own"

    def move(step):
        src = source_of(step)
        for other in (0, 1):
            expert = across if other else e
            for p in range(len(PIECES)):
                if late(other, p):
                    continue
                arrival = piece_copy(3, src, expert, other, p, {"expert": sibling})
                if other:
                    arrival.wait_recv()
                else:
                    @pl.when(step > 0)
                    def _():
                        arrival.wait_recv()
                each_send(step, src, other, p, lambda c: c.start())

    def cross(step):
        src = source_of(step)
        for p in range(len(PIECES)):
            if late(1, p):
                piece_copy(3, src, across, 1, p, {"expert": sibling}).wait_recv()
                each_send(step, src, 1, p, lambda c: c.start())

    def await_sibling(step):
        src = source_of(step)
        for other in (0, 1):
            expert = (sibling + 2) % 4 if other else sibling
            for p in range(len(PIECES)):
                piece_copy(3, src, expert, other, p, {"expert": sibling}).wait_recv()

    def compute(step):
        src = source_of(step)
        wide = lax.broadcasted_iota(jnp.int32, (group_rows, LANES), 1)
        gate = jnp.sum(
            jnp.where(wide == e, blocks[src, :, 2 * width:2 * width + LANES].astype(F32), 0.0),
            axis=1, keepdims=True,
        )
        mine = pl.ds(pl.multiple_of(z * shard, LANES), shard)
        mine_og = pl.ds(pl.multiple_of(width + z * shard, LANES), shard)
        gate_sum[...] = jnp.zeros_like(gate_sum)

        def h_step(i, carry):
            hs = pl.ds(pl.multiple_of(i * H_TILE, H_TILE), H_TILE)
            x = blocks[src, :, 0:width]
            pre_gate = jnp.dot(x, wg[:, hs], preferred_element_type=F32)
            pre_up = jnp.dot(x, wu[:, hs], preferred_element_type=F32)
            back = dot_nt(blocks[src, :, width:2 * width], wd[hs, :])
            sig = jax.nn.sigmoid(pre_gate)
            act = pre_gate * sig
            hidden = (act * pre_up).astype(BF16)
            gate_sum[...] += jnp.sum(hidden.astype(F32) * back, axis=1, keepdims=True)
            scaled = gate * back
            grad_g = (scaled * pre_up * sig * (1.0 + pre_gate * (1.0 - sig))).astype(BF16)
            grad_u = (scaled * act).astype(BF16)
            keep_g[:, hs] = grad_g
            keep_u[:, hs] = grad_u
            xs = blocks[src, :, mine]
            acc_g[:, hs] += dot_tn(xs, grad_g)
            acc_u[:, hs] += dot_tn(xs, grad_u)
            scaled_grad = (gate * blocks[src, :, mine_og].astype(F32)).astype(BF16)
            acc_d[hs, :] += dot_tn(hidden, scaled_grad)
            return carry

        lax.fori_loop(0, hidden_width // H_TILE, h_step, 0)

    def give_copy(j):
        return pltpu.make_async_remote_copy(
            src_ref=give.at[(e + j) % 4], dst_ref=got.at[j - 1],
            send_sem=give_sem.at[j - 1], recv_sem=got_sem.at[j - 1],
            device_id={"expert": (e + j) % 4}, device_id_type=MESH,
        )

    def route_back():
        def d_step(i, carry):
            ds = pl.ds(pl.multiple_of(i * D_TILE, D_TILE), D_TILE)
            total = dot_nt(keep_g[...], wg[ds, :]) + dot_nt(keep_u[...], wu[ds, :])
            give[:, :, ds] = total.astype(BF16).reshape(n_expert, rows, D_TILE)
            return carry

        lax.fori_loop(0, width // D_TILE, d_step, 0)
        give[:, :, width:width + LANES] = (
            jnp.broadcast_to(gate_sum[...], (group_rows, LANES))
            .astype(BF16).reshape(n_expert, rows, LANES)
        )
        for j in (1, 2, 3):
            give_copy(j).start()

    def one_turn(turn, carry):
        @pl.when(turn < n_dp)
        def _():
            move(turn)

        @pl.when(turn == 0)
        def _():
            acc_g[...] = jnp.zeros_like(acc_g)
            acc_u[...] = jnp.zeros_like(acc_u)
            acc_d[...] = jnp.zeros_like(acc_d)
            for load in loads[2:]:
                load.wait()

        @pl.when(turn > 0)
        def _():
            step = turn - 1
            cross(step)
            await_sibling(step)
            compute(step)

        @pl.when(turn == 1)
        def _():
            route_back()

        return carry

    lax.fori_loop(0, n_dp + 1, one_turn, 0)

    for j in (1, 2, 3):
        give_copy(j).wait_recv()
    total = give[e, :, 0:width].astype(F32)
    for j in (1, 2, 3):
        total += got[j - 1, :, 0:width].astype(F32)
    gtok_out[...] = total.astype(BF16)
    picked = []
    for k in range(2):
        route = routes_ref[:, k:k + 1]
        value = jnp.where(route == e, give[e, :, width:width + LANES].astype(F32), 0.0)
        for j in (1, 2, 3):
            value += jnp.where(
                route == (e + 4 - j) % 4, got[j - 1, :, width:width + LANES].astype(F32), 0.0
            )
        picked.append(value)
    ggate_out[...] = jnp.where(lane == 0, picked[0], picked[1])[:, 0:2].astype(BF16)
    dg_out[0] = acc_g[...].astype(BF16)
    du_out[0] = acc_u[...].astype(BF16)
    dd_out[0] = acc_d[...].astype(BF16)

    def drain(step, carry):
        src = source_of(step)
        for other in (0, 1):
            for p in range(len(PIECES)):
                each_send(step, src, other, p, lambda c: c.wait_send())
        return carry

    lax.fori_loop(0, n_dp, drain, 0)
    for j in (1, 2, 3):
        give_copy(j).wait_send()


def gathered_body(tokens, out_grad, routes, route_gates, w_gate, w_up, w_down):
    n_expert, n_dp = lax.axis_size("expert"), lax.axis_size("dp")
    rows, width = tokens.shape
    hid = w_gate.shape[2]
    shard = width // n_dp
    group_rows = n_expert * rows
    vmem = pl.BlockSpec(memory_space=pltpu.VMEM)
    hbm = pl.BlockSpec(memory_space=pl.ANY)
    pieces = len(PIECES)
    return pl.pallas_call(
        functools.partial(layer_kernel, n_expert, n_dp),
        out_shape=(
            jax.ShapeDtypeStruct((rows, width), BF16),
            jax.ShapeDtypeStruct((rows, 2), BF16),
            jax.ShapeDtypeStruct((1, shard, hid), BF16),
            jax.ShapeDtypeStruct((1, shard, hid), BF16),
            jax.ShapeDtypeStruct((1, hid, shard), BF16),
        ),
        in_specs=[hbm, hbm, vmem, vmem, hbm, hbm, hbm],
        out_specs=(vmem,) * 5,
        scratch_shapes=[
            pltpu.VMEM((n_dp, group_rows, 2 * width + LANES), BF16),
            pltpu.VMEM((width, hid), BF16),
            pltpu.VMEM((width, hid), BF16),
            pltpu.VMEM((hid, width), BF16),
            pltpu.VMEM((shard, hid), F32),
            pltpu.VMEM((shard, hid), F32),
            pltpu.VMEM((hid, shard), F32),
            pltpu.VMEM((group_rows, hid), BF16),
            pltpu.VMEM((group_rows, hid), BF16),
            pltpu.VMEM((group_rows, 1), F32),
            pltpu.VMEM((n_expert, rows, width + LANES), BF16),
            pltpu.VMEM((n_expert - 1, rows, width + LANES), BF16),
            pltpu.SemaphoreType.DMA((5,)),
            pltpu.SemaphoreType.DMA((4, n_dp, 2, pieces)),
            pltpu.SemaphoreType.DMA((n_dp, n_expert, pieces)),
            pltpu.SemaphoreType.DMA((3,)),
            pltpu.SemaphoreType.DMA((3,)),
        ],
        compiler_params=pltpu.CompilerParams(
            collective_id=0, has_side_effects=True, vmem_limit_bytes=60 * 2**20
        ),
    )(tokens, out_grad, routes, route_gates, w_gate, w_up, w_down)


def expert_rows(token_rows, grad_rows, gate_rows, gate_mat, up_mat, down_mat):
    pre_gate = jnp.dot(token_rows, gate_mat, preferred_element_type=jnp.float32)
    pre_up = jnp.dot(token_rows, up_mat, preferred_element_type=jnp.float32)
    sigmoid_gate = jax.nn.sigmoid(pre_gate)
    activated = pre_gate * sigmoid_gate
    hidden = (activated * pre_up).astype(jnp.bfloat16)
    back_proj = jnp.einsum("rd,hd->rh", grad_rows, down_mat, preferred_element_type=jnp.float32)
    expert_output = jnp.dot(hidden, down_mat, preferred_element_type=jnp.float32)
    gate_grad = jnp.sum(expert_output * grad_rows.astype(jnp.float32), axis=1)
    gate_scale = gate_rows.astype(jnp.float32)[:, None]
    scaled_back = gate_scale * back_proj
    grad_pre_gate = (
        scaled_back * pre_up * sigmoid_gate * (1.0 + pre_gate * (1.0 - sigmoid_gate))
    ).astype(jnp.bfloat16)
    grad_pre_up = (scaled_back * activated).astype(jnp.bfloat16)
    route_grad = (
        jnp.einsum("rh,dh->rd", grad_pre_gate, gate_mat, preferred_element_type=jnp.float32)
        + jnp.einsum("rh,dh->rd", grad_pre_up, up_mat, preferred_element_type=jnp.float32)
    ).astype(jnp.bfloat16)
    scaled_grad = (gate_scale * grad_rows.astype(jnp.float32)).astype(jnp.bfloat16)
    return (
        route_grad,
        gate_grad.astype(jnp.bfloat16),
        grad_pre_gate,
        grad_pre_up,
        hidden,
        scaled_grad,
    )


def body(tokens, out_grad, routes, route_gates, w_gate, w_up, w_down):
    tok_count, top_count = routes.shape
    model_width = tokens.shape[1]
    experts_total = lax.axis_size("expert")
    route_count = tok_count * top_count
    capacity = 2 * route_count // experts_total
    slot_total = experts_total * capacity
    flat_ids = routes.reshape(-1)
    one_hot = (flat_ids[:, None] == jnp.arange(experts_total, dtype=jnp.int32)[None, :]).astype(
        jnp.int32
    )
    route_rank = jnp.sum(jnp.cumsum(one_hot, axis=0) * one_hot, axis=1) - 1
    slot_index = flat_ids * capacity + route_rank
    slot_owner = (
        jnp.full((slot_total,), route_count, jnp.int32)
        .at[slot_index]
        .set(jnp.arange(route_count, dtype=jnp.int32))
    )
    filled = slot_owner < route_count
    safe_owner = jnp.minimum(slot_owner, route_count - 1)
    token_pick = safe_owner // top_count
    zero_bf = jnp.zeros((), jnp.bfloat16)
    send_tokens = jnp.where(filled[:, None], tokens[token_pick], zero_bf).reshape(
        experts_total, capacity, model_width
    )
    send_grads = jnp.where(filled[:, None], out_grad[token_pick], zero_bf).reshape(
        experts_total, capacity, model_width
    )
    send_gates = jnp.where(filled, route_gates.reshape(-1)[safe_owner], zero_bf).reshape(
        experts_total, capacity
    )
    recv_tokens, recv_grads, recv_gates = (
        lax.all_to_all(send_tokens, "expert", split_axis=0, concat_axis=0, tiled=True),
        lax.all_to_all(send_grads, "expert", split_axis=0, concat_axis=0, tiled=True),
        lax.all_to_all(send_gates, "expert", split_axis=0, concat_axis=0, tiled=True),
    )
    slot_rows = recv_tokens.shape[0] * recv_tokens.shape[1]
    token_rows = recv_tokens.reshape(slot_rows, model_width)
    grad_rows = recv_grads.reshape(slot_rows, model_width)
    gate_rows = recv_gates.reshape(slot_rows)
    gate_mat = w_gate[0]
    up_mat = w_up[0]
    down_mat = w_down[0]
    route_grad, gate_grad, grad_pre_gate, grad_pre_up, hidden, scaled_grad = expert_rows(
        token_rows, grad_rows, gate_rows, gate_mat, up_mat, down_mat
    )
    back_grad, back_gate = (
        lax.all_to_all(
            route_grad.reshape(experts_total, capacity, model_width),
            "expert",
            split_axis=0,
            concat_axis=0,
            tiled=True,
        ),
        lax.all_to_all(
            gate_grad.reshape(experts_total, capacity),
            "expert",
            split_axis=0,
            concat_axis=0,
            tiled=True,
        ),
    )
    home_grad = back_grad.reshape(slot_total, model_width)[slot_index]
    grad_tokens = jnp.sum(
        home_grad.reshape(tok_count, top_count, model_width).astype(jnp.float32), axis=1
    ).astype(jnp.bfloat16)
    grad_gates = back_gate.reshape(slot_total)[slot_index].reshape(tok_count, top_count)
    term_gate = jnp.einsum(
        "rd,rh->dh", token_rows, grad_pre_gate, preferred_element_type=jnp.float32
    )
    term_up = jnp.einsum("rd,rh->dh", token_rows, grad_pre_up, preferred_element_type=jnp.float32)
    term_down = jnp.einsum("rh,rd->hd", hidden, scaled_grad, preferred_element_type=jnp.float32)
    shares = (
        lax.psum_scatter(term_gate, "dp", scatter_dimension=0, tiled=True),
        lax.psum_scatter(term_up, "dp", scatter_dimension=0, tiled=True),
        lax.psum_scatter(term_down, "dp", scatter_dimension=1, tiled=True),
    )
    grad_gate = shares[0].astype(jnp.bfloat16)[None]
    grad_up = shares[1].astype(jnp.bfloat16)[None]
    grad_down = shares[2].astype(jnp.bfloat16)[None]
    return (grad_tokens, grad_gates, grad_gate, grad_up, grad_down)


def solution(mesh):
    placed = (
        P(("groups", "expert", "dp"), None),
        P(("groups", "expert", "dp"), None),
        P(("groups", "expert", "dp"), None),
        P(("groups", "expert", "dp"), None),
        P("expert", None, None),
        P("expert", None, None),
        P("expert", None, None),
    )
    small = mesh.shape["expert"] == 4 and mesh.shape["dp"] == 4
    return jax.shard_map(
        gathered_body if small else body,
        mesh=mesh,
        in_specs=placed,
        out_specs=(
            P(("groups", "expert", "dp"), None),
            P(("groups", "expert", "dp"), None),
            P(("groups", "expert"), "dp", None),
            P(("groups", "expert"), "dp", None),
            P(("groups", "expert"), None, "dp"),
        ),
        check_vma=False,
    )
```

```python
import functools
import jax
import jax.numpy as jnp
from jax import lax
from jax.experimental import pallas as pl
from jax.experimental.pallas import tpu as pltpu
from jax.sharding import PartitionSpec as P

MESH = pl.DeviceIdType.MESH
F32 = jnp.float32
BF16 = jnp.bfloat16
LANES = 128
PIECES = ((0, 32, "both"), (32, 48, "own"), (80, 48, "own"))
H_TILE = 256
D_TILE = 256


def dot_nt(a, b):
    return lax.dot_general(a, b, (((1,), (1,)), ((), ())), preferred_element_type=F32)


def dot_tn(a, b):
    return lax.dot_general(a, b, (((0,), (0,)), ((), ())), preferred_element_type=F32)


def layer_kernel(
    n_expert, n_dp,
    tok_ref, og_ref, packed_ref, wg_hbm, wu_hbm, wd_hbm,
    gtok_out, ggate_out, dg_out, du_out, dd_out,
    blocks, wg, wu, wd, acc_g, acc_u, acc_d, keep_g, keep_u, gate_sum, give, got,
    load_sem, send_sem, recv_sem, give_sem, got_sem,
):
    rows = tok_ref.shape[0]
    width = tok_ref.shape[1]
    hidden_width = wg.shape[1]
    group_rows = n_expert * rows
    shard = width // n_dp
    e = lax.axis_index("expert")
    z = lax.axis_index("dp")
    core = e % 2
    sibling = e + 1 - 2 * core
    across = (e + 2) % 4

    def own_rows(expert, start, count):
        return pl.ds(pl.multiple_of(expert * rows + start, 16), count)

    loads = [
        pltpu.make_async_copy(tok_ref, blocks.at[z, own_rows(e, 0, rows), 0:width], load_sem.at[0]),
        pltpu.make_async_copy(og_ref, blocks.at[z, own_rows(e, 0, rows), width:2 * width], load_sem.at[1]),
        pltpu.make_async_copy(wg_hbm.at[0], wg, load_sem.at[2]),
        pltpu.make_async_copy(wu_hbm.at[0], wu, load_sem.at[3]),
        pltpu.make_async_copy(wd_hbm.at[0], wd, load_sem.at[4]),
    ]
    for load in loads:
        load.start()

    barrier = pltpu.get_barrier_semaphore()
    for j in (1, 2, 3):
        pl.semaphore_signal(barrier, inc=1, device_id={"expert": (e + j) % 4}, device_id_type=MESH)

    @pl.when(z > 0)
    def _():
        pl.semaphore_signal(barrier, inc=1, device_id={"dp": z - 1}, device_id_type=MESH)

    @pl.when(z < n_dp - 1)
    def _():
        pl.semaphore_signal(barrier, inc=1, device_id={"dp": z + 1}, device_id_type=MESH)

    lane = lax.broadcasted_iota(jnp.int32, (rows, LANES), 1)
    spread = jnp.zeros((rows, LANES), F32)
    for k in range(2):
        spread += jnp.where(
            lane == packed_ref[:, k:k + 1].astype(jnp.int32), packed_ref[:, 2 + k:3 + k], 0.0
        )
    blocks[z, own_rows(e, 0, rows), 2 * width:2 * width + LANES] = spread.astype(BF16)

    pl.semaphore_wait(barrier, 3 + jnp.minimum(z, 1) + jnp.minimum(n_dp - 1 - z, 1))

    loads[0].wait()
    loads[1].wait()

    def source_of(step):
        half = z // 2
        near = z + half * (3 - 2 * z)
        last = step // 3
        inner = last * 3 + (1 - last) * ((step + 1) % 3)
        place = (1 - near) * step + near * inner
        return place + half * (3 - 2 * place)

    def piece_copy(kind, src, expert, other, p, target):
        start, count, _ = PIECES[p]
        ref = blocks.at[src, own_rows(expert, start, count), :]
        return pltpu.make_async_remote_copy(
            src_ref=ref, dst_ref=ref,
            send_sem=send_sem.at[kind, src, other, p],
            recv_sem=recv_sem.at[src, expert, p],
            device_id=target, device_id_type=MESH,
        )

    def each_send(step, src, other, p, act):
        expert = across if other else e
        both = PIECES[p][2] == "both"
        if both or not other:
            @pl.when(jnp.logical_and(src <= z, z < n_dp - 1))
            def _():
                act(piece_copy(0, src, expert, other, p, {"dp": z + 1}))

            @pl.when(jnp.logical_and(src >= z, z > 0))
            def _():
                act(piece_copy(1, src, expert, other, p, {"dp": z - 1}))
        if not other:
            if both:
                @pl.when(step == 0)
                def _():
                    act(piece_copy(2, src, expert, other, p, {"expert": across}))
            else:
                act(piece_copy(2, src, expert, other, p, {"expert": across}))
        act(piece_copy(3, src, expert, other, p, {"expert": sibling}))

    def late(other, p):
        return other == 1 and PIECES[p][2] == "own"

    def move(step):
        src = source_of(step)
        for other in (0, 1):
            expert = across if other else e
            for p in range(len(PIECES)):
                if late(other, p):
                    continue
                arrival = piece_copy(3, src, expert, other, p, {"expert": sibling})
                if other:
                    arrival.wait_recv()
                else:
                    @pl.when(step > 0)
                    def _():
                        arrival.wait_recv()
                each_send(step, src, other, p, lambda c: c.start())

    def cross(step):
        src = source_of(step)
        for p in range(len(PIECES)):
            if late(1, p):
                piece_copy(3, src, across, 1, p, {"expert": sibling}).wait_recv()
                each_send(step, src, 1, p, lambda c: c.start())

    def await_sibling(step):
        src = source_of(step)
        for other in (0, 1):
            expert = (sibling + 2) % 4 if other else sibling
            for p in range(len(PIECES)):
                piece_copy(3, src, expert, other, p, {"expert": sibling}).wait_recv()

    def compute(step):
        src = source_of(step)
        wide = lax.broadcasted_iota(jnp.int32, (group_rows, LANES), 1)
        gate = jnp.sum(
            jnp.where(wide == e, blocks[src, :, 2 * width:2 * width + LANES].astype(F32), 0.0),
            axis=1, keepdims=True,
        )
        mine = pl.ds(pl.multiple_of(z * shard, LANES), shard)
        mine_og = pl.ds(pl.multiple_of(width + z * shard, LANES), shard)
        gate_sum[...] = jnp.zeros_like(gate_sum)

        def h_step(i, carry):
            hs = pl.ds(pl.multiple_of(i * H_TILE, H_TILE), H_TILE)
            x = blocks[src, :, 0:width]
            pre_gate = jnp.dot(x, wg[:, hs], preferred_element_type=F32)
            pre_up = jnp.dot(x, wu[:, hs], preferred_element_type=F32)
            back = dot_nt(blocks[src, :, width:2 * width], wd[hs, :])
            sig = jax.nn.sigmoid(pre_gate)
            act = pre_gate * sig
            hidden = (act * pre_up).astype(BF16)
            gate_sum[...] += jnp.sum(hidden.astype(F32) * back, axis=1, keepdims=True)
            scaled = gate * back
            grad_g = (scaled * pre_up * sig * (1.0 + pre_gate * (1.0 - sig))).astype(BF16)
            grad_u = (scaled * act).astype(BF16)
            keep_g[:, hs] = grad_g
            keep_u[:, hs] = grad_u
            xs = blocks[src, :, mine]
            acc_g[:, hs] += dot_tn(xs, grad_g)
            acc_u[:, hs] += dot_tn(xs, grad_u)
            scaled_grad = (gate * blocks[src, :, mine_og].astype(F32)).astype(BF16)
            acc_d[hs, :] += dot_tn(hidden, scaled_grad)
            return carry

        lax.fori_loop(0, hidden_width // H_TILE, h_step, 0)

    def give_copy(j):
        return pltpu.make_async_remote_copy(
            src_ref=give.at[(e + j) % 4], dst_ref=got.at[j - 1],
            send_sem=give_sem.at[j - 1], recv_sem=got_sem.at[j - 1],
            device_id={"expert": (e + j) % 4}, device_id_type=MESH,
        )

    def route_back():
        def d_step(i, carry):
            ds = pl.ds(pl.multiple_of(i * D_TILE, D_TILE), D_TILE)
            total = dot_nt(keep_g[...], wg[ds, :]) + dot_nt(keep_u[...], wu[ds, :])
            give[:, :, ds] = total.astype(BF16).reshape(n_expert, rows, D_TILE)
            return carry

        lax.fori_loop(0, width // D_TILE, d_step, 0)
        give[:, :, width:width + LANES] = (
            jnp.broadcast_to(gate_sum[...], (group_rows, LANES))
            .astype(BF16).reshape(n_expert, rows, LANES)
        )
        for j in (1, 2, 3):
            give_copy(j).start()

    def home():
        for j in (1, 2, 3):
            give_copy(j).wait_recv()
        total = give[e, :, 0:width].astype(F32)
        for j in (1, 2, 3):
            total += got[j - 1, :, 0:width].astype(F32)
        gtok_out[...] = total.astype(BF16)
        picked = []
        for k in range(2):
            route = packed_ref[:, k:k + 1].astype(jnp.int32)
            value = jnp.where(route == e, give[e, :, width:width + LANES].astype(F32), 0.0)
            for j in (1, 2, 3):
                value += jnp.where(
                    route == (e + 4 - j) % 4, got[j - 1, :, width:width + LANES].astype(F32), 0.0
                )
            picked.append(value)
        ggate_out[...] = jnp.where(lane == 0, picked[0], picked[1])[:, 0:2].astype(BF16)

    def one_turn(turn, carry):
        @pl.when(turn < n_dp)
        def _():
            move(turn)

        @pl.when(turn == 0)
        def _():
            acc_g[...] = jnp.zeros_like(acc_g)
            acc_u[...] = jnp.zeros_like(acc_u)
            acc_d[...] = jnp.zeros_like(acc_d)
            for load in loads[2:]:
                load.wait()

        @pl.when(turn > 0)
        def _():
            step = turn - 1
            cross(step)
            await_sibling(step)
            compute(step)

        @pl.when(turn == 1)
        def _():
            route_back()

        @pl.when(turn == n_dp - 1)
        def _():
            home()

        return carry

    lax.fori_loop(0, n_dp + 1, one_turn, 0)

    dg_out[0] = acc_g[...].astype(BF16)
    du_out[0] = acc_u[...].astype(BF16)
    dd_out[0] = acc_d[...].astype(BF16)

    def drain(step, carry):
        src = source_of(step)
        for other in (0, 1):
            for p in range(len(PIECES)):
                each_send(step, src, other, p, lambda c: c.wait_send())
        return carry

    lax.fori_loop(0, n_dp, drain, 0)
    for j in (1, 2, 3):
        give_copy(j).wait_send()


def gathered_body(tokens, out_grad, routes, route_gates, w_gate, w_up, w_down):
    n_expert, n_dp = lax.axis_size("expert"), lax.axis_size("dp")
    rows, width = tokens.shape
    hid = w_gate.shape[2]
    shard = width // n_dp
    group_rows = n_expert * rows
    vmem = pl.BlockSpec(memory_space=pltpu.VMEM)
    hbm = pl.BlockSpec(memory_space=pl.ANY)
    pieces = len(PIECES)
    packed = jnp.concatenate([routes.astype(F32), route_gates.astype(F32)], axis=1)
    return pl.pallas_call(
        functools.partial(layer_kernel, n_expert, n_dp),
        out_shape=(
            jax.ShapeDtypeStruct((rows, width), BF16),
            jax.ShapeDtypeStruct((rows, 2), BF16),
            jax.ShapeDtypeStruct((1, shard, hid), BF16),
            jax.ShapeDtypeStruct((1, shard, hid), BF16),
            jax.ShapeDtypeStruct((1, hid, shard), BF16),
        ),
        in_specs=[hbm, hbm, vmem, hbm, hbm, hbm],
        out_specs=(vmem,) * 5,
        scratch_shapes=[
            pltpu.VMEM((n_dp, group_rows, 2 * width + LANES), BF16),
            pltpu.VMEM((width, hid), BF16),
            pltpu.VMEM((width, hid), BF16),
            pltpu.VMEM((hid, width), BF16),
            pltpu.VMEM((shard, hid), F32),
            pltpu.VMEM((shard, hid), F32),
            pltpu.VMEM((hid, shard), F32),
            pltpu.VMEM((group_rows, hid), BF16),
            pltpu.VMEM((group_rows, hid), BF16),
            pltpu.VMEM((group_rows, 1), F32),
            pltpu.VMEM((n_expert, rows, width + LANES), BF16),
            pltpu.VMEM((n_expert - 1, rows, width + LANES), BF16),
            pltpu.SemaphoreType.DMA((5,)),
            pltpu.SemaphoreType.DMA((4, n_dp, 2, pieces)),
            pltpu.SemaphoreType.DMA((n_dp, n_expert, pieces)),
            pltpu.SemaphoreType.DMA((3,)),
            pltpu.SemaphoreType.DMA((3,)),
        ],
        compiler_params=pltpu.CompilerParams(
            collective_id=0, has_side_effects=True, vmem_limit_bytes=60 * 2**20
        ),
    )(tokens, out_grad, packed, w_gate, w_up, w_down)


def expert_rows(token_rows, grad_rows, gate_rows, gate_mat, up_mat, down_mat):
    pre_gate = jnp.dot(token_rows, gate_mat, preferred_element_type=jnp.float32)
    pre_up = jnp.dot(token_rows, up_mat, preferred_element_type=jnp.float32)
    sigmoid_gate = jax.nn.sigmoid(pre_gate)
    activated = pre_gate * sigmoid_gate
    hidden = (activated * pre_up).astype(jnp.bfloat16)
    back_proj = jnp.einsum("rd,hd->rh", grad_rows, down_mat, preferred_element_type=jnp.float32)
    expert_output = jnp.dot(hidden, down_mat, preferred_element_type=jnp.float32)
    gate_grad = jnp.sum(expert_output * grad_rows.astype(jnp.float32), axis=1)
    gate_scale = gate_rows.astype(jnp.float32)[:, None]
    scaled_back = gate_scale * back_proj
    grad_pre_gate = (
        scaled_back * pre_up * sigmoid_gate * (1.0 + pre_gate * (1.0 - sigmoid_gate))
    ).astype(jnp.bfloat16)
    grad_pre_up = (scaled_back * activated).astype(jnp.bfloat16)
    route_grad = (
        jnp.einsum("rh,dh->rd", grad_pre_gate, gate_mat, preferred_element_type=jnp.float32)
        + jnp.einsum("rh,dh->rd", grad_pre_up, up_mat, preferred_element_type=jnp.float32)
    ).astype(jnp.bfloat16)
    scaled_grad = (gate_scale * grad_rows.astype(jnp.float32)).astype(jnp.bfloat16)
    return (
        route_grad,
        gate_grad.astype(jnp.bfloat16),
        grad_pre_gate,
        grad_pre_up,
        hidden,
        scaled_grad,
    )


def body(tokens, out_grad, routes, route_gates, w_gate, w_up, w_down):
    tok_count, top_count = routes.shape
    model_width = tokens.shape[1]
    experts_total = lax.axis_size("expert")
    route_count = tok_count * top_count
    capacity = 2 * route_count // experts_total
    slot_total = experts_total * capacity
    flat_ids = routes.reshape(-1)
    one_hot = (flat_ids[:, None] == jnp.arange(experts_total, dtype=jnp.int32)[None, :]).astype(
        jnp.int32
    )
    route_rank = jnp.sum(jnp.cumsum(one_hot, axis=0) * one_hot, axis=1) - 1
    slot_index = flat_ids * capacity + route_rank
    slot_owner = (
        jnp.full((slot_total,), route_count, jnp.int32)
        .at[slot_index]
        .set(jnp.arange(route_count, dtype=jnp.int32))
    )
    filled = slot_owner < route_count
    safe_owner = jnp.minimum(slot_owner, route_count - 1)
    token_pick = safe_owner // top_count
    zero_bf = jnp.zeros((), jnp.bfloat16)
    send_tokens = jnp.where(filled[:, None], tokens[token_pick], zero_bf).reshape(
        experts_total, capacity, model_width
    )
    send_grads = jnp.where(filled[:, None], out_grad[token_pick], zero_bf).reshape(
        experts_total, capacity, model_width
    )
    send_gates = jnp.where(filled, route_gates.reshape(-1)[safe_owner], zero_bf).reshape(
        experts_total, capacity
    )
    recv_tokens, recv_grads, recv_gates = (
        lax.all_to_all(send_tokens, "expert", split_axis=0, concat_axis=0, tiled=True),
        lax.all_to_all(send_grads, "expert", split_axis=0, concat_axis=0, tiled=True),
        lax.all_to_all(send_gates, "expert", split_axis=0, concat_axis=0, tiled=True),
    )
    slot_rows = recv_tokens.shape[0] * recv_tokens.shape[1]
    token_rows = recv_tokens.reshape(slot_rows, model_width)
    grad_rows = recv_grads.reshape(slot_rows, model_width)
    gate_rows = recv_gates.reshape(slot_rows)
    gate_mat = w_gate[0]
    up_mat = w_up[0]
    down_mat = w_down[0]
    route_grad, gate_grad, grad_pre_gate, grad_pre_up, hidden, scaled_grad = expert_rows(
        token_rows, grad_rows, gate_rows, gate_mat, up_mat, down_mat
    )
    back_grad, back_gate = (
        lax.all_to_all(
            route_grad.reshape(experts_total, capacity, model_width),
            "expert",
            split_axis=0,
            concat_axis=0,
            tiled=True,
        ),
        lax.all_to_all(
            gate_grad.reshape(experts_total, capacity),
            "expert",
            split_axis=0,
            concat_axis=0,
            tiled=True,
        ),
    )
    home_grad = back_grad.reshape(slot_total, model_width)[slot_index]
    grad_tokens = jnp.sum(
        home_grad.reshape(tok_count, top_count, model_width).astype(jnp.float32), axis=1
    ).astype(jnp.bfloat16)
    grad_gates = back_gate.reshape(slot_total)[slot_index].reshape(tok_count, top_count)
    term_gate = jnp.einsum(
        "rd,rh->dh", token_rows, grad_pre_gate, preferred_element_type=jnp.float32
    )
    term_up = jnp.einsum("rd,rh->dh", token_rows, grad_pre_up, preferred_element_type=jnp.float32)
    term_down = jnp.einsum("rh,rd->hd", hidden, scaled_grad, preferred_element_type=jnp.float32)
    shares = (
        lax.psum_scatter(term_gate, "dp", scatter_dimension=0, tiled=True),
        lax.psum_scatter(term_up, "dp", scatter_dimension=0, tiled=True),
        lax.psum_scatter(term_down, "dp", scatter_dimension=1, tiled=True),
    )
    grad_gate = shares[0].astype(jnp.bfloat16)[None]
    grad_up = shares[1].astype(jnp.bfloat16)[None]
    grad_down = shares[2].astype(jnp.bfloat16)[None]
    return (grad_tokens, grad_gates, grad_gate, grad_up, grad_down)


def solution(mesh):
    placed = (
        P(("groups", "expert", "dp"), None),
        P(("groups", "expert", "dp"), None),
        P(("groups", "expert", "dp"), None),
        P(("groups", "expert", "dp"), None),
        P("expert", None, None),
        P("expert", None, None),
        P("expert", None, None),
    )
    small = mesh.shape["expert"] == 4 and mesh.shape["dp"] == 4
    return jax.shard_map(
        gathered_body if small else body,
        mesh=mesh,
        in_specs=placed,
        out_specs=(
            P(("groups", "expert", "dp"), None),
            P(("groups", "expert", "dp"), None),
            P(("groups", "expert"), "dp", None),
            P(("groups", "expert"), "dp", None),
            P(("groups", "expert"), None, "dp"),
        ),
        check_vma=False,
    )
```
